512 devices in a mesh: band: 64 (over z_lo, y, core), grid: 8 (over x, z_hi).
Axes of the slice: x: 4, y: 4, z: 16 (z_hi: 2, z_lo: 8; z = z_hi * 8 + z_lo), core: 2. Of those that a mesh axis runs over, the one named last changes fastest.
Arguments:
- bands: float32 [256, 80, 6400], P('band', 'grid'), may hold values from -6 to 6
- pair_list: int32 [64, 2, 1, 2], P('band'), may hold values from 0 to 3
Outputs:
- exchange_action: float32 [256, 80, 6400], P('band', 'grid')
The draws below stay inside these ranges and needn't reach their ends.
Inputs may be any that keep to these rules, and one draw needn't show every extreme that they name: `pair_list`: band indices within a block.
All inputs are finite; a program needn't handle non-finite values.
Results may differ from the reference program's by a relative error of at most 0.0001.
Values sent between devices are 32-bit elements; how exact they have to be, the bound alone decides.
A program may use at most 64 MiB of HBM per device.

```python
import math
import jax
import jax.numpy as jnp
from jax import lax

NG = 80
BAND_DEV = 4
SHIFTS = 2
PAIRS = 1
BANDS = 256
N_BAND = 64


def plant(result, key, smallest, high):
    longest = result.shape.index(max(result.shape))
    spots = []
    for shift in (0, 1):
        where = [jax.random.randint(jax.random.fold_in(key, axis), (), 0, length) for axis, length in enumerate(result.shape)]
        where[longest] = (where[longest] + shift) % result.shape[longest]
        spots.append(tuple(where))
    return result.at[spots[0]].set(smallest).at[spots[1]].set(high)


def block_levels(key, extent, cuts, least, top_value):
    factor_of, own = 1.0, jax.random.fold_in(key, 6)
    for axis_at, parts in cuts:
        draws = jnp.exp(jax.random.uniform(jax.random.fold_in(own, axis_at), (parts,), jnp.float32, least / len(cuts), top_value / len(cuts)))
        factor_of = factor_of * jnp.repeat(draws, extent[axis_at] // parts).reshape([-1 if axis == axis_at else 1 for axis in range(len(extent))])
    return factor_of


def bell_draw(key, shape, width, limit, shards=(), kind=jnp.bfloat16):
    factor_of = block_levels(key, shape, shards, -0.22, 0.18) if shards else 1.0
    values = jax.random.normal(key, shape, jnp.float32) * width * factor_of
    return jnp.minimum(jnp.maximum(values, -limit), limit).astype(kind)


def setup_inputs(seed: int = 0) -> dict:
    keys = jax.random.split(jax.random.key(seed), 3)
    bands = bell_draw(keys[0], (BANDS, NG, NG * NG), 1.0, 6.0, ((0, 64), (1, 8)), jnp.float32)
    pair_list = plant(jax.random.randint(keys[1], (N_BAND, SHIFTS, PAIRS, 2), 0, BAND_DEV), jax.random.fold_in(keys[1], 1), 0, BAND_DEV - 1).astype(jnp.int32)
    return dict(bands=bands, pair_list=pair_list)


coupling = 1.0
screen = 0.1


def squared_wave(frequency):
    wrapped = jnp.where(frequency > NG // 2, frequency - NG, frequency)
    waves = wrapped.astype(jnp.float32) * (2.0 * math.pi / NG)
    return waves * waves


def reference(bands, pair_list):
    points = jnp.arange(NG, dtype=jnp.int32)
    squared = squared_wave(points)
    inner = squared[: NG // 2 + 1]
    kernel = coupling / (squared[:, None, None] + squared[None, :, None] + inner[None, None, :] + screen * screen)
    blocks = jnp.arange(N_BAND, dtype=jnp.int32)[:, None, None]
    shifts = jnp.arange(1, SHIFTS + 1, dtype=jnp.int32)[None, :, None]
    first_rows = (blocks * BAND_DEV + pair_list[..., 0]).reshape(-1).astype(jnp.int32)
    second_rows = (((blocks + shifts) % N_BAND) * BAND_DEV + pair_list[..., 1]).reshape(-1).astype(jnp.int32)
    field = bands.reshape(BANDS, NG, NG, NG)

    def accumulate(action, pair):
        first, second = pair
        own_band = field[first]
        far_band = field[second]
        spectrum = jnp.fft.rfftn(own_band * far_band) * kernel
        potential = jnp.fft.irfftn(spectrum, s=(NG, NG, NG)).astype(jnp.float32)
        action = action.at[first].add(-potential * far_band)
        action = action.at[second].add(-potential * own_band)
        return action, None

    action, _ = lax.scan(accumulate, jnp.zeros((BANDS, NG, NG, NG), jnp.float32), (first_rows, second_rows))
    return action.reshape(BANDS, NG, NG * NG)
```

```python
import math

import jax
import jax.numpy as jnp
import ml_dtypes
import numpy as np
from jax import lax
from jax.experimental import pallas as pl
from jax.experimental.pallas import tpu as pltpu
from jax.sharding import PartitionSpec as P

NG = 80
SCREEN = 0.1
MESH = pl.DeviceIdType.MESH
ROWS = 104
BIG, SMALL = 7, 6


def row_of(a, x):
    return 8 * a + x if x < 8 else 80 + 2 * a + x - 8


def plane_of(source, x):
    return 8 * source + x if x < 8 else 64 + 2 * source + x - 8


def halves(table):
    table = np.asarray(table, np.float64)
    high = table.astype(np.float32).astype(ml_dtypes.bfloat16)
    low = (table - high.astype(np.float64)).astype(np.float32).astype(ml_dtypes.bfloat16)
    return np.stack([high, low])


def wave(k):
    k = np.where(k > NG // 2, k - NG, k)
    return (k * (2.0 * math.pi / NG)) ** 2


def complex_map(table):
    out = np.zeros((2, table.shape[0], 2, table.shape[1]))
    out[0, :, 0], out[1, :, 0] = table.real, -table.imag
    out[0, :, 1], out[1, :, 1] = table.imag, table.real
    return out


def tables():
    z = np.arange(NG)
    into = np.zeros((8, NG, 6, 128))
    back = np.zeros((6, 128, 8, NG))
    for r in range(8):
        for kz in range(40):
            g, j = divmod(kz, 8)
            angle = 2 * math.pi * (kz * z % NG) / NG
            weight = 1.0 if kz == 0 else 2.0
            into[r, :, g, j * 8 + r] = np.cos(angle)
            into[r, :, g, 64 + j * 8 + r] = -np.sin(angle)
            back[g, j * 8 + r, r] = weight * np.cos(angle)
            back[g, 64 + j * 8 + r, r] = -weight * np.sin(angle)
        sign = 1.0 - 2.0 * (z % 2)
        for lane in range(r, 128, 8):
            into[r, :, 5, lane] = sign
            back[5, lane, r] = sign
    along_y = np.zeros((2, ROWS, 112))
    for k in range(10):
        for a in range(10):
            angle = 2 * math.pi * (k * a % 10) / 10
            for x in range(10):
                along_y[0, row_of(k, x), row_of(a, x)] = math.cos(angle)
                along_y[1, row_of(k, x), row_of(a, x)] = math.sin(angle)
    along_x = np.zeros((2, NG, NG))
    k = np.arange(NG)
    for source in range(8):
        for x in range(10):
            angle = 2 * math.pi * (k * (10 * source + x) % NG) / NG
            along_x[0, :, plane_of(source, x)] = np.cos(angle)
            along_x[1, :, plane_of(source, x)] = np.sin(angle)
    along_x = along_x.reshape(160, NG)
    fine = np.zeros((12, 2, 128, 128))
    fine_back = np.zeros((12, 128, 2, 128))
    waves = np.zeros((56, 128))
    r = np.arange(8)
    for k1 in range(10):
        ky = k1 + 10 * np.arange(8)
        phase = 2 * math.pi * (r[:, None] * ky[None, :] % NG) / NG
        table = np.exp(-1j * phase)
        forward = [complex_map(table), complex_map(-1j * table)]
        inverse = [complex_map(np.conj(table).T), complex_map(1j * np.conj(table).T)]
        for part in range(2):
            for c in range(2):
                for d in range(2):
                    for j in range(8):
                        fine[k1, part, c * 64 + j * 8 : c * 64 + j * 8 + 8, d * 64 + j * 8 : d * 64 + j * 8 + 8] = forward[part][c, :, d]
                        fine_back[k1, c * 64 + j * 8 : c * 64 + j * 8 + 8, part, d * 64 + j * 8 : d * 64 + j * 8 + 8] = inverse[part][c, :, d]
                    last, at = 10 + k1 // 8, k1 % 8 * 16
                    fine[last, part, at + c * 8 : at + c * 8 + 8, at + d * 8 : at + d * 8 + 8] = forward[part][c, :, d]
                    fine_back[last, at + c * 8 : at + c * 8 + 8, part, at + d * 8 : at + d * 8 + 8] = inverse[part][c, :, d]
        for c in range(2):
            for kz in range(40):
                at = c * 64 + kz % 8 * 8
                waves[kz // 8 * 10 + k1, at : at + 8] = wave(ky) + wave(np.array(kz))
            at = k1 % 8 * 16 + c * 8
            waves[50 + k1 // 8, at : at + 8] = wave(ky) + wave(np.array(40))
    wave_x = np.broadcast_to(wave(k)[:, None], (NG, 128))
    return (
        halves(into.reshape(640, 768)),
        halves(along_y.reshape(2 * ROWS, 112)),
        halves(along_x),
        halves(fine.reshape(12, 256, 128)),
        halves(fine_back.reshape(12, 128, 256)),
        halves(along_x.T),
        halves(back.reshape(768, 640)),
        waves.astype(np.float32),
        np.ascontiguousarray(wave_x).astype(np.float32),
    )


def parts_of(value):
    high = value.astype(jnp.bfloat16)
    return high, (value - high.astype(jnp.float32)).astype(jnp.bfloat16)


def product(a, b):
    def dot(u, v):
        return jnp.dot(u, v, preferred_element_type=jnp.float32)

    return dot(a[0], b[0]) + (dot(a[1], b[0]) + dot(a[0], b[1]))


def table_of(ref):
    return ref[0], ref[1]


def kernel(
    pair_ref, bands_ref, into_c, along_y_c, along_x_c, fine_c, fine_back_c, across_c, back_c, waves_c, wave_x_c,
    out_ref,
    bands, packed, into_t, along_y_t, along_x_t, fine_t, fine_back_t, across_t, back_t, waves_t, wave_x_t,
    band_out, band_in, own, kept, given, taken,
    go_big, go_small, at_big, at_small, ret_big, ret_small, home_big, home_small,
    lines, lines_small, columns,
    load_sem, band_sem, share_sem,
    go_big_sem, go_small_sem, at_big_sem, at_small_sem, ret_big_sem, ret_small_sem, home_big_sem, home_small_sem,
):
    band = lax.axis_index("band")
    grid = lax.axis_index("grid")
    z_low, y_core = lax.div(band, 8), lax.rem(band, 8)
    x_at, z = lax.div(grid, 2), lax.rem(grid, 2) * 8 + lax.div(band, 8)

    def site(x, half):
        far = lax.rem(z_low + 4 + 8 * half, 16)
        return (lax.rem(far, 8) * 8 + y_core, x * 2 + lax.div(far, 8))

    behind = lax.rem(z + 12, 16)
    my_half = lax.div(behind, 8)

    def source(g):
        return (lax.rem(behind, 8) * 8 + y_core, g)

    def neighbour(step):
        return (lax.rem(band + step + 64, 64), grid)

    def remote(src, dst, send, recv, device):
        return pltpu.make_async_remote_copy(
            src_ref=src, dst_ref=dst, send_sem=send, recv_sem=recv, device_id=device, device_id_type=MESH
        )

    loads = [pltpu.make_async_copy(bands_ref, bands, load_sem.at[0])]
    constants = (
        (into_c, into_t), (along_y_c, along_y_t), (along_x_c, along_x_t), (fine_c, fine_t), (fine_back_c, fine_back_t),
        (across_c, across_t), (back_c, back_t), (waves_c, waves_t), (wave_x_c, wave_x_t),
    )
    for number, (src, dst) in enumerate(constants):
        loads.append(pltpu.make_async_copy(src, dst, load_sem.at[number + 1]))
    for load in loads:
        load.start()

    barrier = pltpu.get_barrier_semaphore()
    friends = [neighbour(step) for step in (1, 2, -1, -2)]
    friends += [site(x, half) for half in range(2) for x in range(4)]
    for friend in friends:
        pl.semaphore_signal(barrier, inc=1, device_id=friend, device_id_type=MESH)

    loads[0].wait()

    def pack(k, carry):
        for q in range(5):
            for a in range(10):
                lanes = pl.ds((a * 5 + q) * 128, 128)
                packed[k, q, pl.ds(8 * a, 8), :] = bands[k, 0:8, lanes]
                packed[k, q, pl.ds(80 + 2 * a, 2), :] = bands[k, 8:10, lanes]
            packed[k, q, pl.ds(100, 4), :] = jnp.zeros((4, 128), jnp.float32)
        return carry

    lax.fori_loop(0, 4, pack, 0)
    for p in range(2):
        band_out[p] = packed[pair_ref[0, p, 0, 0]]
        second = pair_ref[0, p, 0, 1].astype(jnp.float32)
        band_out[p, 0, pl.ds(100, 4), :] = jnp.full((4, 128), second, jnp.float32)

    pl.semaphore_wait(barrier, 12)
    shares = [
        remote(band_out.at[p], band_in.at[p], band_sem.at[0, p], band_sem.at[1, p], neighbour(p + 1)) for p in range(2)
    ]
    for share in shares:
        share.start()
    for load in loads[1:]:
        load.wait()

    lane = lax.broadcasted_iota(jnp.int32, (1, 128), 1)
    flip = jnp.where(lane < 64, 1.0, -1.0).astype(jnp.float32)
    real_lane = lax.rem(lax.div(lane, 8), 2) == 0
    slot_lane = lax.div(lane, 16)
    nothing = jnp.zeros((8, 128), jnp.float32)

    def places(p):
        for x in range(4):
            first = BIG if p == 0 else SMALL
            for j in range(13):
                big = (j < first) == (p == 0)
                yield 13 * x + j, x, big, j if j < first else j - first

    def targets(p):
        for x in range(4):
            yield x, True, p
            yield x, False, 1 - p

    def going(p, x, big, half):
        if big:
            return remote(go_big.at[p, x], at_big.at[grid], go_big_sem.at[p, x], at_big_sem.at[grid], site(x, half))
        return remote(go_small.at[p, x], at_small.at[grid], go_small_sem.at[p, x], at_small_sem.at[grid], site(x, half))

    def returning(g, big):
        if big:
            return remote(
                ret_big.at[g], home_big.at[my_half, x_at], ret_big_sem.at[g], home_big_sem.at[my_half, x_at], source(g)
            )
        return remote(
            ret_small.at[g], home_small.at[1 - my_half, x_at], ret_small_sem.at[g], home_small_sem.at[1 - my_half, x_at],
            source(g),
        )

    def forward(p):
        shares[p].wait_recv()
        wanted = band_in[p, 0, pl.ds(100, 1), :]
        density = []
        for q in range(5):
            mine = packed[3, q]
            for k in range(3):
                mine = jnp.where(wanted == float(k), packed[k, q], mine)
            own[p, q] = mine
            density.append(jnp.concatenate([band_in[p, q] * mine, nothing], axis=0))
        rows = product(parts_of(jnp.concatenate(density, axis=1)), table_of(into_t))
        both = product(table_of(along_y_t), parts_of(rows))
        tiles = []
        for g in range(5):
            span = slice(g * 128, g * 128 + 128)
            tiles.append(both[:ROWS, span] + flip * pltpu.roll(both[ROWS:, span], 64, 1))
        last = jnp.where(real_lane, both[:ROWS, 640:], -both[ROWS:, 640:])
        for tile, x, big, j in places(p):
            buffer, size = (go_big, BIG) if big else (go_small, SMALL)
            g, k = divmod(tile, 10)
            if g < 5:
                main = tiles[g][8 * k : 8 * k + 8]
                rest = tiles[g][80 + 2 * k : 82 + 2 * k]
            else:
                main = jnp.zeros((8, 128), jnp.float32)
                rest = jnp.zeros((2, 128), jnp.float32)
                for k1 in range(8 * k, min(8 * k + 8, 10)):
                    here = slot_lane == k1 - 8 * k
                    main = jnp.where(here, last[8 * k1 : 8 * k1 + 8], main)
                    rest = jnp.where(here, last[80 + 2 * k1 : 82 + 2 * k1], rest)
            buffer[p, x, pl.ds(8 * j, 8), :] = main
            buffer[p, x, pl.ds(8 * size + 2 * j, 2), :] = rest
        for x, big, half in targets(p):
            going(p, x, big, half).start()

    def middle(big):
        size = BIG if big else SMALL
        arrived, arrived_sem, sent = (at_big, at_big_sem, ret_big) if big else (at_small, at_small_sem, ret_small)
        buffer = lines if big else lines_small
        start = 13 * x_at + (6 if big else 7) * my_half
        for g in range(8):
            remote(arrived.at[g], arrived.at[g], arrived_sem.at[g], arrived_sem.at[g], source(g)).wait_recv()
        for j in range(size):
            for g in range(8):
                buffer[pl.ds(8 * g, 8), pl.ds(128 * j, 128)] = arrived[g, pl.ds(8 * j, 8), :]
                buffer[pl.ds(64 + 2 * g, 2), pl.ds(128 * j, 128)] = arrived[g, pl.ds(8 * size + 2 * j, 2), :]
        waved = product(table_of(along_x_t), parts_of(buffer[...]))
        ups, downs = [], []
        for j in range(size):
            span = slice(128 * j, 128 * j + 128)
            tile = start + j
            which = lax.rem(tile, 10) + 10 * lax.div(tile, 50)
            pair = jnp.concatenate([waved[:NG, span], waved[NG:, span]], axis=1)
            spectrum = product(parts_of(pair), (fine_t[0, which], fine_t[1, which]))
            total = wave_x_t[...] + waves_t[pl.ds(tile, 1), :] + SCREEN * SCREEN
            spectrum = spectrum * ((1.0 / NG**3) / total)
            pair = product(parts_of(spectrum), (fine_back_t[0, which], fine_back_t[1, which]))
            ups.append(pair[:, :128])
            downs.append(pair[:, 128:])
        stacked = jnp.concatenate([jnp.concatenate(ups, axis=1), jnp.concatenate(downs, axis=1)], axis=0)
        result = product(table_of(across_t), parts_of(stacked))
        for g in range(8):
            for j in range(size):
                span = slice(128 * j, 128 * j + 128)
                sent[g, pl.ds(8 * j, 8), :] = result[8 * g : 8 * g + 8, span]
                sent[g, pl.ds(8 * size + 2 * j, 2), :] = result[64 + 2 * g : 66 + 2 * g, span]
            returning(g, big).start()

    def giving(p, q):
        return remote(
            given.at[p, q], taken.at[p, q], share_sem.at[0, p, q], share_sem.at[1, p, q], neighbour(-p - 1)
        )

    def backward(p):
        for x, big, half in targets(p):
            home, home_sem = (home_big, home_big_sem) if big else (home_small, home_small_sem)
            remote(home.at[p, x], home.at[p, x], home_sem.at[p, x], home_sem.at[p, x], site(x, half)).wait_recv()
        for tile, x, big, j in places(p):
            home, size = (home_big, BIG) if big else (home_small, SMALL)
            main = home[p, x, pl.ds(8 * j, 8), :]
            rest = home[p, x, pl.ds(8 * size + 2 * j, 2), :]
            g, k = divmod(tile, 10)
            if g < 5:
                columns[pl.ds(8 * k, 8), pl.ds(128 * g, 128)] = main
                columns[pl.ds(80 + 2 * k, 2), pl.ds(128 * g, 128)] = rest
            else:
                for k1 in range(8 * k, min(8 * k + 8, 10)):
                    here = slot_lane == k1 - 8 * k
                    columns[pl.ds(8 * k1, 8), pl.ds(640, 128)] = jnp.where(here, main, 0.0)
                    columns[pl.ds(80 + 2 * k1, 2), pl.ds(640, 128)] = jnp.where(here, rest, 0.0)
        both = product(table_of(along_y_t), parts_of(columns[...]))
        tiles = []
        for g in range(5):
            span = slice(g * 128, g * 128 + 128)
            tiles.append(both[:ROWS, span] - flip * pltpu.roll(both[ROWS:, span], 64, 1))
        tiles.append(jnp.where(real_lane, both[:ROWS, 640:], -both[ROWS:, 640:]))
        rows = parts_of(jnp.concatenate([jnp.concatenate(tiles, axis=1), jnp.zeros((8, 768), jnp.float32)], axis=0))
        for q in range(5):
            span = pl.ds(128 * q, 128)
            potential = product(rows, (back_t[0, :, span], back_t[1, :, span]))[:ROWS]
            kept[p, q] = potential * band_in[p, q]
            given[p, q] = (potential * own[p, q])[:100]
            giving(p, q).start()

    columns[pl.ds(96, 16), :] = jnp.zeros((16, 768), jnp.float32)
    forward(0)
    forward(1)
    pl.when(my_half == 0)(lambda: middle(True))
    middle(False)
    pl.when(my_half == 1)(lambda: middle(True))
    backward(0)
    backward(1)

    seconds = [band_in[p, 0, pl.ds(100, 1), :] for p in range(2)]
    for q in range(5):
        for p in range(2):
            giving(p, q).wait_recv()
        for k in range(4):
            total = jnp.zeros((100, 128), jnp.float32)
            for p in range(2):
                total = total - jnp.where(seconds[p] == float(k), kept[p, q, pl.ds(0, 100), :], 0.0)
                total = total - jnp.where(pair_ref[0, p, 0, 0] == k, taken[p, q], 0.0)
            for a in range(10):
                lanes = pl.ds((a * 5 + q) * 128, 128)
                out_ref[k, 0:8, lanes] = total[8 * a : 8 * a + 8]
                out_ref[k, 8:10, lanes] = total[80 + 2 * a : 82 + 2 * a]

    for p in range(2):
        shares[p].wait_send()
        for x, big, half in targets(p):
            going(p, x, big, half).wait_send()
        for q in range(5):
            giving(p, q).wait_send()
    for g in range(8):
        returning(g, True).wait_send()
        returning(g, False).wait_send()


def body(bands, pair_list):
    constants = [jnp.asarray(table) for table in tables()]
    f32 = jnp.float32
    dma = pltpu.SemaphoreType.DMA
    scratch = [pltpu.VMEM((4, 10, 6400), f32), pltpu.VMEM((4, 5, ROWS, 128), f32)]
    scratch += [pltpu.VMEM(table.shape, table.dtype) for table in constants]
    scratch += [pltpu.VMEM((2, 5, ROWS, 128), f32)] * 4
    scratch += [pltpu.VMEM((2, 5, 100, 128), f32)] * 2
    big, small = 10 * BIG, 10 * SMALL
    scratch += [pltpu.VMEM((2, 4, big, 128), f32), pltpu.VMEM((2, 4, small, 128), f32)]
    scratch += [pltpu.VMEM((8, big, 128), f32), pltpu.VMEM((8, small, 128), f32)] * 2
    scratch += [pltpu.VMEM((2, 4, big, 128), f32), pltpu.VMEM((2, 4, small, 128), f32)]
    scratch += [pltpu.VMEM((NG, 128 * BIG), f32), pltpu.VMEM((NG, 128 * SMALL), f32), pltpu.VMEM((112, 768), f32)]
    scratch += [dma((10,)), dma((2, 2)), dma((2, 2, 5))]
    scratch += [dma((2, 4))] * 2 + [dma((8,))] * 4 + [dma((2, 4))] * 2
    return pl.pallas_call(
        kernel,
        out_shape=jax.ShapeDtypeStruct(bands.shape, f32),
        in_specs=[pl.BlockSpec(memory_space=pltpu.SMEM)] + [pl.BlockSpec(memory_space=pl.ANY)] * 10,
        out_specs=pl.BlockSpec(memory_space=pltpu.VMEM),
        scratch_shapes=scratch,
        compiler_params=pltpu.CompilerParams(collective_id=0, has_side_effects=True, vmem_limit_bytes=48 * 2**20),
        name="exchange",
    )(pair_list, bands, *constants)


def solution(mesh):
    in_specs = (P("band", "grid", None), P("band", None, None, None))
    out_specs = P("band", "grid", None)
    return jax.shard_map(body, mesh=mesh, in_specs=in_specs, out_specs=out_specs, check_vma=False)
```

```python
import math

import jax
import jax.numpy as jnp
import ml_dtypes
import numpy as np
from jax import lax
from jax.experimental import pallas as pl
from jax.experimental.pallas import tpu as pltpu
from jax.sharding import PartitionSpec as P

NG = 80
SCREEN = 0.1
MESH = pl.DeviceIdType.MESH
ROWS = 104
BIG, SMALL = 7, 6


def row_of(a, x):
    return 8 * a + x if x < 8 else 80 + 2 * a + x - 8


def plane_of(source, x):
    return 8 * source + x if x < 8 else 64 + 2 * source + x - 8


def halves(table):
    table = np.asarray(table, np.float64)
    high = table.astype(np.float32).astype(ml_dtypes.bfloat16)
    low = (table - high.astype(np.float64)).astype(np.float32).astype(ml_dtypes.bfloat16)
    return np.stack([high, low])


def wave(k):
    k = np.where(k > NG // 2, k - NG, k)
    return (k * (2.0 * math.pi / NG)) ** 2


def complex_map(table):
    out = np.zeros((2, table.shape[0], 2, table.shape[1]))
    out[0, :, 0], out[1, :, 0] = table.real, -table.imag
    out[0, :, 1], out[1, :, 1] = table.imag, table.real
    return out


def tables():
    z = np.arange(NG)
    into = np.zeros((8, NG, 6, 128))
    back = np.zeros((6, 128, 8, NG))
    for r in range(8):
        for kz in range(40):
            g, j = divmod(kz, 8)
            angle = 2 * math.pi * (kz * z % NG) / NG
            weight = 1.0 if kz == 0 else 2.0
            into[r, :, g, j * 8 + r] = np.cos(angle)
            into[r, :, g, 64 + j * 8 + r] = -np.sin(angle)
            back[g, j * 8 + r, r] = weight * np.cos(angle)
            back[g, 64 + j * 8 + r, r] = -weight * np.sin(angle)
        sign = 1.0 - 2.0 * (z % 2)
        for lane in range(r, 128, 8):
            into[r, :, 5, lane] = sign
            back[5, lane, r] = sign
    along_y = np.zeros((2, ROWS, 112))
    for k in range(10):
        for a in range(10):
            angle = 2 * math.pi * (k * a % 10) / 10
            for x in range(10):
                along_y[0, row_of(k, x), row_of(a, x)] = math.cos(angle)
                along_y[1, row_of(k, x), row_of(a, x)] = math.sin(angle)
    along_x = np.zeros((2, NG, NG))
    k = np.arange(NG)
    for source in range(8):
        for x in range(10):
            angle = 2 * math.pi * (k * (10 * source + x) % NG) / NG
            along_x[0, :, plane_of(source, x)] = np.cos(angle)
            along_x[1, :, plane_of(source, x)] = np.sin(angle)
    along_x = along_x.reshape(160, NG)
    fine = np.zeros((12, 2, 128, 128))
    fine_back = np.zeros((12, 128, 2, 128))
    waves = np.zeros((56, 128))
    r = np.arange(8)
    for k1 in range(10):
        ky = k1 + 10 * np.arange(8)
        phase = 2 * math.pi * (r[:, None] * ky[None, :] % NG) / NG
        table = np.exp(-1j * phase)
        forward = [complex_map(table), complex_map(-1j * table)]
        inverse = [complex_map(np.conj(table).T), complex_map(1j * np.conj(table).T)]
        for part in range(2):
            for c in range(2):
                for d in range(2):
                    for j in range(8):
                        fine[k1, part, c * 64 + j * 8 : c * 64 + j * 8 + 8, d * 64 + j * 8 : d * 64 + j * 8 + 8] = forward[part][c, :, d]
                        fine_back[k1, c * 64 + j * 8 : c * 64 + j * 8 + 8, part, d * 64 + j * 8 : d * 64 + j * 8 + 8] = inverse[part][c, :, d]
                    last, at = 10 + k1 // 8, k1 % 8 * 16
                    fine[last, part, at + c * 8 : at + c * 8 + 8, at + d * 8 : at + d * 8 + 8] = forward[part][c, :, d]
                    fine_back[last, at + c * 8 : at + c * 8 + 8, part, at + d * 8 : at + d * 8 + 8] = inverse[part][c, :, d]
        for c in range(2):
            for kz in range(40):
                at = c * 64 + kz % 8 * 8
                waves[kz // 8 * 10 + k1, at : at + 8] = wave(ky) + wave(np.array(kz))
            at = k1 % 8 * 16 + c * 8
            waves[50 + k1 // 8, at : at + 8] = wave(ky) + wave(np.array(40))
    wave_x = np.broadcast_to(wave(k)[:, None], (NG, 128))
    return (
        halves(into.reshape(640, 768)),
        halves(along_y.reshape(2 * ROWS, 112)),
        halves(along_x),
        halves(fine.reshape(12, 256, 128)),
        halves(fine_back.reshape(12, 128, 256)),
        halves(along_x.T),
        halves(back.reshape(768, 640)),
        waves.astype(np.float32),
        np.ascontiguousarray(wave_x).astype(np.float32),
    )


def parts_of(value):
    high = value.astype(jnp.bfloat16)
    return high, (value - high.astype(jnp.float32)).astype(jnp.bfloat16)


def product(a, b):
    def dot(u, v):
        return jnp.dot(u, v, preferred_element_type=jnp.float32)

    return dot(a[0], b[0]) + (dot(a[1], b[0]) + dot(a[0], b[1]))


def table_of(ref):
    return ref[0], ref[1]


def kernel(
    pair_ref, bands_ref, into_c, along_y_c, along_x_c, fine_c, fine_back_c, across_c, back_c, waves_c, wave_x_c,
    out_ref,
    bands, staged, packed, into_t, along_y_t, along_x_t, fine_t, fine_back_t, across_t, back_t, waves_t, wave_x_t,
    band_out, band_in, index_out, index_in, own, kept, given, taken,
    go_big, go_small, at_big, at_small, ret_big, ret_small, home_big, home_small,
    lines, lines_small, columns,
    load_sem, band_sem, index_sem, share_sem,
    go_big_sem, go_small_sem, at_big_sem, at_small_sem, ret_big_sem, ret_small_sem, home_big_sem, home_small_sem,
):
    band = lax.axis_index("band")
    grid = lax.axis_index("grid")
    z_low, y_core = lax.div(band, 8), lax.rem(band, 8)
    x_at, z = lax.div(grid, 2), lax.rem(grid, 2) * 8 + lax.div(band, 8)

    def site(x, half):
        far = lax.rem(z_low + 4 + 8 * half, 16)
        return (lax.rem(far, 8) * 8 + y_core, x * 2 + lax.div(far, 8))

    behind = lax.rem(z + 12, 16)
    my_half = lax.div(behind, 8)

    def source(g):
        return (lax.rem(behind, 8) * 8 + y_core, g)

    def neighbour(step):
        return (lax.rem(band + step + 64, 64), grid)

    def remote(src, dst, send, recv, device):
        return pltpu.make_async_remote_copy(
            src_ref=src, dst_ref=dst, send_sem=send, recv_sem=recv, device_id=device, device_id_type=MESH
        )

    loads = [pltpu.make_async_copy(bands_ref, bands, load_sem.at[0])]
    constants = (
        (into_c, into_t), (along_y_c, along_y_t), (along_x_c, along_x_t), (fine_c, fine_t), (fine_back_c, fine_back_t),
        (across_c, across_t), (back_c, back_t), (waves_c, waves_t), (wave_x_c, wave_x_t),
    )
    for number, (src, dst) in enumerate(constants):
        loads.append(pltpu.make_async_copy(src, dst, load_sem.at[number + 1]))
    for load in loads:
        load.start()

    barrier = pltpu.get_barrier_semaphore()
    friends = [neighbour(step) for step in (1, 2, -1, -2)]
    friends += [site(x, half) for half in range(2) for x in range(4)]
    for friend in friends:
        pl.semaphore_signal(barrier, inc=1, device_id=friend, device_id_type=MESH)

    loads[0].wait()

    def stage(t, carry):
        lanes = pl.ds(pl.multiple_of(t * 128, 128), 128)
        for x in range(10):
            staged[pl.ds(pl.multiple_of(t * 40 + 4 * x, 4), 4), :] = bands[x, :, lanes]
        return carry

    lax.fori_loop(0, 50, stage, 0, unroll=5)

    def pack(k, carry):
        for q in range(5):
            for a in range(10):
                first = (a * 5 + q) * 40 + k
                packed[k, q, pl.ds(8 * a, 8), :] = staged[pl.ds(first, 8, stride=4), :]
                packed[k, q, pl.ds(80 + 2 * a, 2), :] = staged[pl.ds(first + 32, 2, stride=4), :]
            packed[k, q, pl.ds(100, 4), :] = jnp.zeros((4, 128), jnp.float32)
        return carry

    lax.fori_loop(0, 4, pack, 0)
    band_out[0] = packed[pair_ref[0, 0, 0, 0]]
    band_out[0, 0, pl.ds(100, 4), :] = jnp.full((4, 128), pair_ref[0, 0, 0, 1].astype(jnp.float32), jnp.float32)
    index_out[...] = jnp.full((8, 128), pair_ref[0, 1, 0, 1].astype(jnp.float32), jnp.float32)

    pl.semaphore_wait(barrier, 12)
    steps = (1, 2 - 4 * lax.rem(band, 2))
    shares = [
        remote(band_out.at[p], band_in.at[p], band_sem.at[0, p], band_sem.at[1, p], neighbour(steps[p])) for p in range(2)
    ]
    notice = remote(index_out, index_in, index_sem.at[0], index_sem.at[1], neighbour(2))
    shares[0].start()
    notice.start()
    for load in loads[1:]:
        load.wait()

    lane = lax.broadcasted_iota(jnp.int32, (1, 128), 1)
    flip = jnp.where(lane < 64, 1.0, -1.0).astype(jnp.float32)
    real_lane = lax.rem(lax.div(lane, 8), 2) == 0
    slot_lane = lax.div(lane, 16)
    nothing = jnp.zeros((8, 128), jnp.float32)

    def chosen(index, q):
        value = packed[3, q]
        for k in range(3):
            value = jnp.where(index == float(k), packed[k, q], value)
        return value

    def roles(p):
        ours = jnp.full((1, 128), pair_ref[0, p, 0, 0].astype(jnp.float32), jnp.float32)
        if p == 0:
            return ours, band_in[0, 0, pl.ds(100, 1), :]
        theirs = index_in[pl.ds(0, 1), :]
        here = lax.rem(band, 2) == 0
        return jnp.where(here, ours, theirs), jnp.where(here, theirs, ours)

    def places(p):
        for x in range(4):
            first = BIG if p == 0 else SMALL
            for j in range(13):
                big = (j < first) == (p == 0)
                yield 13 * x + j, x, big, j if j < first else j - first

    def targets(p):
        for x in range(4):
            yield x, True, p
            yield x, False, 1 - p

    def going(p, x, big, half):
        if big:
            return remote(go_big.at[p, x], at_big.at[grid], go_big_sem.at[p, x], at_big_sem.at[grid], site(x, half))
        return remote(go_small.at[p, x], at_small.at[grid], go_small_sem.at[p, x], at_small_sem.at[grid], site(x, half))

    def returning(g, big):
        if big:
            return remote(
                ret_big.at[g], home_big.at[my_half, x_at], ret_big_sem.at[g], home_big_sem.at[my_half, x_at], source(g)
            )
        return remote(
            ret_small.at[g], home_small.at[1 - my_half, x_at], ret_small_sem.at[g], home_small_sem.at[1 - my_half, x_at],
            source(g),
        )

    def forward(p):
        shares[p].wait_recv()
        wanted = roles(p)[1]
        density = []
        for q in range(5):
            mine = chosen(wanted, q)
            own[p, q] = mine
            density.append(jnp.concatenate([band_in[p, q] * mine, nothing], axis=0))
        rows = product(parts_of(jnp.concatenate(density, axis=1)), table_of(into_t))
        both = product(table_of(along_y_t), parts_of(rows))
        tiles = []
        for g in range(5):
            span = slice(g * 128, g * 128 + 128)
            tiles.append(both[:ROWS, span] + flip * pltpu.roll(both[ROWS:, span], 64, 1))
        last = jnp.where(real_lane, both[:ROWS, 640:], -both[ROWS:, 640:])
        for tile, x, big, j in places(p):
            buffer, size = (go_big, BIG) if big else (go_small, SMALL)
            g, k = divmod(tile, 10)
            if g < 5:
                main = tiles[g][8 * k : 8 * k + 8]
                rest = tiles[g][80 + 2 * k : 82 + 2 * k]
            else:
                main = jnp.zeros((8, 128), jnp.float32)
                rest = jnp.zeros((2, 128), jnp.float32)
                for k1 in range(8 * k, min(8 * k + 8, 10)):
                    here = slot_lane == k1 - 8 * k
                    main = jnp.where(here, last[8 * k1 : 8 * k1 + 8], main)
                    rest = jnp.where(here, last[80 + 2 * k1 : 82 + 2 * k1], rest)
            buffer[p, x, pl.ds(8 * j, 8), :] = main
            buffer[p, x, pl.ds(8 * size + 2 * j, 2), :] = rest
        for x, big, half in targets(p):
            going(p, x, big, half).start()

    def arrive(big):
        arrived, arrived_sem = (at_big, at_big_sem) if big else (at_small, at_small_sem)
        for g in range(8):
            remote(arrived.at[g], arrived.at[g], arrived_sem.at[g], arrived_sem.at[g], source(g)).wait_recv()

    def leave(big):
        for g in range(8):
            returning(g, big).start()

    def middle(big):
        size = BIG if big else SMALL
        arrived, sent = (at_big, ret_big) if big else (at_small, ret_small)
        buffer = lines if big else lines_small
        start = 13 * x_at + (6 if big else 7) * my_half
        for j in range(size):
            for g in range(8):
                buffer[pl.ds(8 * g, 8), pl.ds(128 * j, 128)] = arrived[g, pl.ds(8 * j, 8), :]
                buffer[pl.ds(64 + 2 * g, 2), pl.ds(128 * j, 128)] = arrived[g, pl.ds(8 * size + 2 * j, 2), :]
        waved = product(table_of(along_x_t), parts_of(buffer[...]))
        ups, downs = [], []
        for j in range(size):
            span = slice(128 * j, 128 * j + 128)
            tile = start + j
            which = lax.rem(tile, 10) + 10 * lax.div(tile, 50)
            pair = jnp.concatenate([waved[:NG, span], waved[NG:, span]], axis=1)
            spectrum = product(parts_of(pair), (fine_t[0, which], fine_t[1, which]))
            total = wave_x_t[...] + waves_t[pl.ds(tile, 1), :] + SCREEN * SCREEN
            spectrum = spectrum * ((1.0 / NG**3) / total)
            pair = product(parts_of(spectrum), (fine_back_t[0, which], fine_back_t[1, which]))
            ups.append(pair[:, :128])
            downs.append(pair[:, 128:])
        stacked = jnp.concatenate([jnp.concatenate(ups, axis=1), jnp.concatenate(downs, axis=1)], axis=0)
        result = product(table_of(across_t), parts_of(stacked))
        for g in range(8):
            for j in range(size):
                span = slice(128 * j, 128 * j + 128)
                sent[g, pl.ds(8 * j, 8), :] = result[8 * g : 8 * g + 8, span]
                sent[g, pl.ds(8 * size + 2 * j, 2), :] = result[64 + 2 * g : 66 + 2 * g, span]

    def giving(p, q):
        return remote(
            given.at[p, q], taken.at[p, q], share_sem.at[0, p, q], share_sem.at[1, p, q], neighbour(-steps[p])
        )

    def backward(p):
        for x, big, half in targets(p):
            home, home_sem = (home_big, home_big_sem) if big else (home_small, home_small_sem)
            remote(home.at[p, x], home.at[p, x], home_sem.at[p, x], home_sem.at[p, x], site(x, half)).wait_recv()
        for tile, x, big, j in places(p):
            home, size = (home_big, BIG) if big else (home_small, SMALL)
            main = home[p, x, pl.ds(8 * j, 8), :]
            rest = home[p, x, pl.ds(8 * size + 2 * j, 2), :]
            g, k = divmod(tile, 10)
            if g < 5:
                columns[pl.ds(8 * k, 8), pl.ds(128 * g, 128)] = main
                columns[pl.ds(80 + 2 * k, 2), pl.ds(128 * g, 128)] = rest
            else:
                for k1 in range(8 * k, min(8 * k + 8, 10)):
                    here = slot_lane == k1 - 8 * k
                    columns[pl.ds(8 * k1, 8), pl.ds(640, 128)] = jnp.where(here, main, 0.0)
                    columns[pl.ds(80 + 2 * k1, 2), pl.ds(640, 128)] = jnp.where(here, rest, 0.0)
        both = product(table_of(along_y_t), parts_of(columns[...]))
        tiles = []
        for g in range(5):
            span = slice(g * 128, g * 128 + 128)
            tiles.append(both[:ROWS, span] - flip * pltpu.roll(both[ROWS:, span], 64, 1))
        tiles.append(jnp.where(real_lane, both[:ROWS, 640:], -both[ROWS:, 640:]))
        rows = parts_of(jnp.concatenate([jnp.concatenate(tiles, axis=1), jnp.zeros((8, 768), jnp.float32)], axis=0))
        for q in range(5):
            span = pl.ds(128 * q, 128)
            potential = product(rows, (back_t[0, :, span], back_t[1, :, span]))[:ROWS]
            kept[p, q] = potential * band_in[p, q]
            given[p, q] = (potential * own[p, q])[:100]
            giving(p, q).start()

    columns[pl.ds(96, 16), :] = jnp.zeros((16, 768), jnp.float32)
    def meet(first):
        arrive(first)
        middle(first)
        arrive(not first)
        leave(first)
        middle(not first)
        leave(not first)

    forward(0)
    notice.wait_recv()
    for q in range(5):
        band_out[1, q] = chosen(roles(1)[0], q)
    shares[1].start()
    forward(1)
    pl.when(my_half == 0)(lambda: meet(True))
    pl.when(my_half == 1)(lambda: meet(False))
    backward(0)
    backward(1)

    moved, stayed = zip(*[roles(p) for p in range(2)])
    for q in range(5):
        for p in range(2):
            giving(p, q).wait_recv()
        for k in range(4):
            total = jnp.zeros((100, 128), jnp.float32)
            for p in range(2):
                total = total - jnp.where(stayed[p] == float(k), kept[p, q, pl.ds(0, 100), :], 0.0)
                total = total - jnp.where(moved[p] == float(k), taken[p, q], 0.0)
            for a in range(10):
                first = (a * 5 + q) * 40 + k
                staged[pl.ds(first, 8, stride=4), :] = total[8 * a : 8 * a + 8]
                staged[pl.ds(first + 32, 2, stride=4), :] = total[80 + 2 * a : 82 + 2 * a]
        for a in range(10):
            t = a * 5 + q
            for x in range(10):
                out_ref[x, :, pl.ds(t * 128, 128)] = staged[pl.ds(t * 40 + 4 * x, 4), :]

    notice.wait_send()
    for p in range(2):
        shares[p].wait_send()
        for x, big, half in targets(p):
            going(p, x, big, half).wait_send()
        for q in range(5):
            giving(p, q).wait_send()
    for g in range(8):
        returning(g, True).wait_send()
        returning(g, False).wait_send()


def body(bands, pair_list):
    constants = [jnp.asarray(table) for table in tables()]
    f32 = jnp.float32
    dma = pltpu.SemaphoreType.DMA
    scratch = [pltpu.VMEM((10, 4, 6400), f32), pltpu.VMEM((2000, 128), f32), pltpu.VMEM((4, 5, ROWS, 128), f32)]
    scratch += [pltpu.VMEM(table.shape, table.dtype) for table in constants]
    scratch += [pltpu.VMEM((2, 5, ROWS, 128), f32)] * 2
    scratch += [pltpu.VMEM((8, 128), f32)] * 2
    scratch += [pltpu.VMEM((2, 5, ROWS, 128), f32)] * 2
    scratch += [pltpu.VMEM((2, 5, 100, 128), f32)] * 2
    big, small = 10 * BIG, 10 * SMALL
    scratch += [pltpu.VMEM((2, 4, big, 128), f32), pltpu.VMEM((2, 4, small, 128), f32)]
    scratch += [pltpu.VMEM((8, big, 128), f32), pltpu.VMEM((8, small, 128), f32)] * 2
    scratch += [pltpu.VMEM((2, 4, big, 128), f32), pltpu.VMEM((2, 4, small, 128), f32)]
    scratch += [pltpu.VMEM((NG, 128 * BIG), f32), pltpu.VMEM((NG, 128 * SMALL), f32), pltpu.VMEM((112, 768), f32)]
    scratch += [dma((10,)), dma((2, 2)), dma((2,)), dma((2, 2, 5))]
    scratch += [dma((2, 4))] * 2 + [dma((8,))] * 4 + [dma((2, 4))] * 2
    lines = bands.transpose(1, 0, 2)
    action = pl.pallas_call(
        kernel,
        out_shape=jax.ShapeDtypeStruct(lines.shape, f32),
        in_specs=[pl.BlockSpec(memory_space=pltpu.SMEM)] + [pl.BlockSpec(memory_space=pl.ANY)] * 10,
        out_specs=pl.BlockSpec(memory_space=pltpu.VMEM),
        scratch_shapes=scratch,
        compiler_params=pltpu.CompilerParams(collective_id=0, has_side_effects=True, vmem_limit_bytes=62 * 2**20),
        name="exchange",
    )(pair_list, lines, *constants)
    return action.transpose(1, 0, 2)


def solution(mesh):
    in_specs = (P("band", "grid", None), P("band", None, None, None))
    out_specs = P("band", "grid", None)
    return jax.shard_map(body, mesh=mesh, in_specs=in_specs, out_specs=out_specs, check_vma=False)
```

```python
import math

import jax
import jax.numpy as jnp
import ml_dtypes
import numpy as np
from jax import lax
from jax.experimental import pallas as pl
from jax.experimental.pallas import tpu as pltpu
from jax.sharding import PartitionSpec as P

NG = 80
SCREEN = 0.1
MESH = pl.DeviceIdType.MESH
ROWS = 104
BIG, SMALL = 7, 6


def row_of(a, x):
    return 8 * a + x if x < 8 else 80 + 2 * a + x - 8


def plane_of(source, x):
    return 8 * source + x if x < 8 else 64 + 2 * source + x - 8


def halves(table):
    table = np.asarray(table, np.float64)
    high = table.astype(np.float32).astype(ml_dtypes.bfloat16)
    low = (table - high.astype(np.float64)).astype(np.float32).astype(ml_dtypes.bfloat16)
    return np.stack([high, low])


def wave(k):
    k = np.where(k > NG // 2, k - NG, k)
    return (k * (2.0 * math.pi / NG)) ** 2


def complex_map(table):
    out = np.zeros((2, table.shape[0], 2, table.shape[1]))
    out[0, :, 0], out[1, :, 0] = table.real, -table.imag
    out[0, :, 1], out[1, :, 1] = table.imag, table.real
    return out


def tables():
    z = np.arange(NG)
    into = np.zeros((8, NG, 6, 128))
    back = np.zeros((6, 128, 8, NG))
    for r in range(8):
        for kz in range(40):
            g, j = divmod(kz, 8)
            angle = 2 * math.pi * (kz * z % NG) / NG
            weight = 1.0 if kz == 0 else 2.0
            into[r, :, g, j * 8 + r] = np.cos(angle)
            into[r, :, g, 64 + j * 8 + r] = -np.sin(angle)
            back[g, j * 8 + r, r] = weight * np.cos(angle)
            back[g, 64 + j * 8 + r, r] = -weight * np.sin(angle)
        sign = 1.0 - 2.0 * (z % 2)
        for lane in range(r, 128, 8):
            into[r, :, 5, lane] = sign
            back[5, lane, r] = sign
    along_y = np.zeros((2, ROWS, 112))
    for k in range(10):
        for a in range(10):
            angle = 2 * math.pi * (k * a % 10) / 10
            for x in range(10):
                along_y[0, row_of(k, x), row_of(a, x)] = math.cos(angle)
                along_y[1, row_of(k, x), row_of(a, x)] = math.sin(angle)
    along_x = np.zeros((2, NG, NG))
    k = np.arange(NG)
    for source in range(8):
        for x in range(10):
            angle = 2 * math.pi * (k * (10 * source + x) % NG) / NG
            along_x[0, :, plane_of(source, x)] = np.cos(angle)
            along_x[1, :, plane_of(source, x)] = np.sin(angle)
    along_x = along_x.reshape(160, NG)
    fine = np.zeros((12, 2, 128, 128))
    fine_back = np.zeros((12, 128, 2, 128))
    waves = np.zeros((56, 128))
    r = np.arange(8)
    for k1 in range(10):
        ky = k1 + 10 * np.arange(8)
        phase = 2 * math.pi * (r[:, None] * ky[None, :] % NG) / NG
        table = np.exp(-1j * phase)
        forward = [complex_map(table), complex_map(-1j * table)]
        inverse = [complex_map(np.conj(table).T), complex_map(1j * np.conj(table).T)]
        for part in range(2):
            for c in range(2):
                for d in range(2):
                    for j in range(8):
                        fine[k1, part, c * 64 + j * 8 : c * 64 + j * 8 + 8, d * 64 + j * 8 : d * 64 + j * 8 + 8] = forward[part][c, :, d]
                        fine_back[k1, c * 64 + j * 8 : c * 64 + j * 8 + 8, part, d * 64 + j * 8 : d * 64 + j * 8 + 8] = inverse[part][c, :, d]
                    last, at = 10 + k1 // 8, k1 % 8 * 16
                    fine[last, part, at + c * 8 : at + c * 8 + 8, at + d * 8 : at + d * 8 + 8] = forward[part][c, :, d]
                    fine_back[last, at + c * 8 : at + c * 8 + 8, part, at + d * 8 : at + d * 8 + 8] = inverse[part][c, :, d]
        for c in range(2):
            for kz in range(40):
                at = c * 64 + kz % 8 * 8
                waves[kz // 8 * 10 + k1, at : at + 8] = wave(ky) + wave(np.array(kz))
            at = k1 % 8 * 16 + c * 8
            waves[50 + k1 // 8, at : at + 8] = wave(ky) + wave(np.array(40))
    wave_x = np.broadcast_to(wave(k)[:, None], (NG, 128))
    return (
        halves(into.reshape(640, 768)),
        halves(along_y.reshape(2 * ROWS, 112)),
        halves(along_x),
        halves(fine.reshape(12, 256, 128)),
        halves(fine_back.reshape(12, 128, 256)),
        halves(along_x.T),
        halves(back.reshape(768, 640)),
        waves.astype(np.float32),
        np.ascontiguousarray(wave_x).astype(np.float32),
    )


def parts_of(value):
    high = value.astype(jnp.bfloat16)
    return high, (value - high.astype(jnp.float32)).astype(jnp.bfloat16)


def product(a, b):
    def dot(u, v):
        return jnp.dot(u, v, preferred_element_type=jnp.float32)

    return dot(a[0], b[0]) + (dot(a[1], b[0]) + dot(a[0], b[1]))


def table_of(ref):
    return ref[0], ref[1]


def kernel(
    pair_ref, bands_ref, into_c, along_y_c, along_x_c, fine_c, fine_back_c, across_c, back_c, waves_c, wave_x_c,
    out_ref,
    bands, staged, packed, into_t, along_y_t, along_x_t, fine_t, fine_back_t, across_t, back_t, waves_t, wave_x_t,
    band_out, band_in, index_out, index_in, own, kept, given, taken,
    go_big, go_small, at_big, at_small, ret_big, ret_small, home_big, home_small,
    lines, lines_small, columns,
    load_sem, band_sem, index_sem, share_sem,
    go_big_sem, go_small_sem, at_big_sem, at_small_sem, ret_big_sem, ret_small_sem, home_big_sem, home_small_sem,
):
    band = lax.axis_index("band")
    grid = lax.axis_index("grid")
    z_low, y_core = lax.div(band, 8), lax.rem(band, 8)
    x_at, z = lax.div(grid, 2), lax.rem(grid, 2) * 8 + lax.div(band, 8)

    def site(x, half):
        far = lax.rem(z_low + 4 + 8 * half, 16)
        return (lax.rem(far, 8) * 8 + y_core, x * 2 + lax.div(far, 8))

    behind = lax.rem(z + 12, 16)
    my_half = lax.div(behind, 8)

    def source(g):
        return (lax.rem(behind, 8) * 8 + y_core, g)

    def neighbour(step):
        return (lax.rem(band + step + 64, 64), grid)

    def remote(src, dst, send, recv, device):
        return pltpu.make_async_remote_copy(
            src_ref=src, dst_ref=dst, send_sem=send, recv_sem=recv, device_id=device, device_id_type=MESH
        )

    loads = [pltpu.make_async_copy(bands_ref, bands, load_sem.at[0])]
    constants = (
        (into_c, into_t), (along_y_c, along_y_t), (along_x_c, along_x_t), (fine_c, fine_t), (fine_back_c, fine_back_t),
        (across_c, across_t), (back_c, back_t), (waves_c, waves_t), (wave_x_c, wave_x_t),
    )
    for number, (src, dst) in enumerate(constants):
        loads.append(pltpu.make_async_copy(src, dst, load_sem.at[number + 1]))
    for load in loads:
        load.start()

    barrier = pltpu.get_barrier_semaphore()
    friends = [neighbour(step) for step in (1, 2, -1, -2)]
    friends += [site(x, half) for half in range(2) for x in range(4)]
    for friend in friends:
        pl.semaphore_signal(barrier, inc=1, device_id=friend, device_id_type=MESH)

    loads[0].wait()

    def stage(t, carry):
        lanes = pl.ds(pl.multiple_of(t * 128, 128), 128)
        for x in range(10):
            staged[pl.ds(pl.multiple_of(t * 40 + 4 * x, 4), 4), :] = bands[x, :, lanes]
        return carry

    lax.fori_loop(0, 50, stage, 0, unroll=5)

    def pack(k, carry):
        for q in range(5):
            for a in range(10):
                first = (a * 5 + q) * 40 + k
                packed[k, q, pl.ds(8 * a, 8), :] = staged[pl.ds(first, 8, stride=4), :]
                packed[k, q, pl.ds(80 + 2 * a, 2), :] = staged[pl.ds(first + 32, 2, stride=4), :]
            packed[k, q, pl.ds(100, 4), :] = jnp.zeros((4, 128), jnp.float32)
        return carry

    lax.fori_loop(0, 4, pack, 0)
    band_out[0] = packed[pair_ref[0, 0, 0, 0]]
    band_out[0, 0, pl.ds(100, 4), :] = jnp.full((4, 128), pair_ref[0, 0, 0, 1].astype(jnp.float32), jnp.float32)
    index_out[...] = jnp.full((8, 128), pair_ref[0, 1, 0, 1].astype(jnp.float32), jnp.float32)

    pl.semaphore_wait(barrier, 12)
    steps = (1, 2 - 4 * lax.rem(band, 2))
    shares = [
        remote(band_out.at[p], band_in.at[p], band_sem.at[0, p], band_sem.at[1, p], neighbour(steps[p])) for p in range(2)
    ]
    notice = remote(index_out, index_in, index_sem.at[0], index_sem.at[1], neighbour(2))
    shares[0].start()
    notice.start()
    for load in loads[1:]:
        load.wait()

    lane = lax.broadcasted_iota(jnp.int32, (1, 128), 1)
    flip = jnp.where(lane < 64, 1.0, -1.0).astype(jnp.float32)
    real_lane = lax.rem(lax.div(lane, 8), 2) == 0
    slot_lane = lax.div(lane, 16)
    nothing = jnp.zeros((8, 128), jnp.float32)

    def chosen(index, q):
        value = packed[3, q]
        for k in range(3):
            value = jnp.where(index == float(k), packed[k, q], value)
        return value

    def roles(p):
        ours = jnp.full((1, 128), pair_ref[0, p, 0, 0].astype(jnp.float32), jnp.float32)
        if p == 0:
            return ours, band_in[0, 0, pl.ds(100, 1), :]
        theirs = index_in[pl.ds(0, 1), :]
        here = lax.rem(band, 2) == 0
        return jnp.where(here, ours, theirs), jnp.where(here, theirs, ours)

    def places(p):
        for x in range(4):
            first = BIG if p == 0 else SMALL
            for j in range(13):
                big = (j < first) == (p == 0)
                yield 13 * x + j, x, big, j if j < first else j - first

    def targets(p):
        for x in range(4):
            yield x, True, p
            yield x, False, 1 - p

    def going(p, x, big, half):
        if big:
            return remote(go_big.at[p, x], at_big.at[grid], go_big_sem.at[p, x], at_big_sem.at[grid], site(x, half))
        return remote(go_small.at[p, x], at_small.at[grid], go_small_sem.at[p, x], at_small_sem.at[grid], site(x, half))

    def returning(g, big):
        if big:
            return remote(
                ret_big.at[g], home_big.at[my_half, x_at], ret_big_sem.at[g], home_big_sem.at[my_half, x_at], source(g)
            )
        return remote(
            ret_small.at[g], home_small.at[1 - my_half, x_at], ret_small_sem.at[g], home_small_sem.at[1 - my_half, x_at],
            source(g),
        )

    def forward(p):
        shares[p].wait_recv()
        wanted = roles(p)[1]
        density = []
        for q in range(5):
            mine = chosen(wanted, q)
            own[p, q] = mine
            density.append(jnp.concatenate([band_in[p, q] * mine, nothing], axis=0))
        rows = product(parts_of(jnp.concatenate(density, axis=1)), table_of(into_t))
        both = product(table_of(along_y_t), parts_of(rows))
        tiles = []
        for g in range(5):
            span = slice(g * 128, g * 128 + 128)
            tiles.append(both[:ROWS, span] + flip * pltpu.roll(both[ROWS:, span], 64, 1))
        last = jnp.where(real_lane, both[:ROWS, 640:], -both[ROWS:, 640:])
        for tile, x, big, j in places(p):
            buffer, size = (go_big, BIG) if big else (go_small, SMALL)
            g, k = divmod(tile, 10)
            if g < 5:
                main = tiles[g][8 * k : 8 * k + 8]
                rest = tiles[g][80 + 2 * k : 82 + 2 * k]
            else:
                main = jnp.zeros((8, 128), jnp.float32)
                rest = jnp.zeros((2, 128), jnp.float32)
                for k1 in range(8 * k, min(8 * k + 8, 10)):
                    here = slot_lane == k1 - 8 * k
                    main = jnp.where(here, last[8 * k1 : 8 * k1 + 8], main)
                    rest = jnp.where(here, last[80 + 2 * k1 : 82 + 2 * k1], rest)
            buffer[p, x, pl.ds(8 * j, 8), :] = main
            buffer[p, x, pl.ds(8 * size + 2 * j, 2), :] = rest
        for x, big, half in targets(p):
            going(p, x, big, half).start()

    def arrive(big):
        arrived, arrived_sem = (at_big, at_big_sem) if big else (at_small, at_small_sem)
        for g in range(8):
            remote(arrived.at[g], arrived.at[g], arrived_sem.at[g], arrived_sem.at[g], source(g)).wait_recv()

    def leave(big):
        for g in range(8):
            returning(g, big).start()

    def middle(big):
        size = BIG if big else SMALL
        arrived, sent = (at_big, ret_big) if big else (at_small, ret_small)
        buffer = lines if big else lines_small
        start = 13 * x_at + (6 if big else 7) * my_half
        for j in range(size):
            for g in range(8):
                buffer[pl.ds(8 * g, 8), pl.ds(128 * j, 128)] = arrived[g, pl.ds(8 * j, 8), :]
                buffer[pl.ds(64 + 2 * g, 2), pl.ds(128 * j, 128)] = arrived[g, pl.ds(8 * size + 2 * j, 2), :]
        waved = product(table_of(along_x_t), parts_of(buffer[...]))
        ups, downs = [], []
        for j in range(size):
            span = slice(128 * j, 128 * j + 128)
            tile = start + j
            which = lax.rem(tile, 10) + 10 * lax.div(tile, 50)
            pair = jnp.concatenate([waved[:NG, span], waved[NG:, span]], axis=1)
            spectrum = product(parts_of(pair), (fine_t[0, which], fine_t[1, which]))
            total = wave_x_t[...] + waves_t[pl.ds(tile, 1), :] + SCREEN * SCREEN
            spectrum = spectrum * ((1.0 / NG**3) / total)
            pair = product(parts_of(spectrum), (fine_back_t[0, which], fine_back_t[1, which]))
            ups.append(pair[:, :128])
            downs.append(pair[:, 128:])
        stacked = jnp.concatenate([jnp.concatenate(ups, axis=1), jnp.concatenate(downs, axis=1)], axis=0)
        result = product(table_of(across_t), parts_of(stacked))
        for g in range(8):
            for j in range(size):
                span = slice(128 * j, 128 * j + 128)
                sent[g, pl.ds(8 * j, 8), :] = result[8 * g : 8 * g + 8, span]
                sent[g, pl.ds(8 * size + 2 * j, 2), :] = result[64 + 2 * g : 66 + 2 * g, span]

    def giving(p, q):
        return remote(
            given.at[p, q], taken.at[p, q], share_sem.at[0, p, q], share_sem.at[1, p, q], neighbour(-steps[p])
        )

    def backward(p):
        for x, big, half in targets(p):
            home, home_sem = (home_big, home_big_sem) if big else (home_small, home_small_sem)
            remote(home.at[p, x], home.at[p, x], home_sem.at[p, x], home_sem.at[p, x], site(x, half)).wait_recv()
        for tile, x, big, j in places(p):
            home, size = (home_big, BIG) if big else (home_small, SMALL)
            main = home[p, x, pl.ds(8 * j, 8), :]
            rest = home[p, x, pl.ds(8 * size + 2 * j, 2), :]
            g, k = divmod(tile, 10)
            if g < 5:
                columns[pl.ds(8 * k, 8), pl.ds(128 * g, 128)] = main
                columns[pl.ds(80 + 2 * k, 2), pl.ds(128 * g, 128)] = rest
            else:
                for k1 in range(8 * k, min(8 * k + 8, 10)):
                    here = slot_lane == k1 - 8 * k
                    columns[pl.ds(8 * k1, 8), pl.ds(640, 128)] = jnp.where(here, main, 0.0)
                    columns[pl.ds(80 + 2 * k1, 2), pl.ds(640, 128)] = jnp.where(here, rest, 0.0)
        both = product(table_of(along_y_t), parts_of(columns[...]))
        tiles = []
        for g in range(5):
            span = slice(g * 128, g * 128 + 128)
            tiles.append(both[:ROWS, span] - flip * pltpu.roll(both[ROWS:, span], 64, 1))
        tiles.append(jnp.where(real_lane, both[:ROWS, 640:], -both[ROWS:, 640:]))
        rows = parts_of(jnp.concatenate([jnp.concatenate(tiles, axis=1), jnp.zeros((8, 768), jnp.float32)], axis=0))
        for q in range(5):
            span = pl.ds(128 * q, 128)
            potential = product(rows, (back_t[0, :, span], back_t[1, :, span]))[:ROWS]
            kept[p, q] = potential * band_in[p, q]
            given[p, q] = (potential * own[p, q])[:100]
            giving(p, q).start()

    columns[pl.ds(96, 16), :] = jnp.zeros((16, 768), jnp.float32)
    later = lax.rem(band, 2) == 1

    def meet(first):
        arrive(first)
        middle(first)
        arrive(not first)
        pl.when(jnp.logical_not(later))(lambda: leave(first))
        middle(not first)
        leave(not first)
        pl.when(later)(lambda: leave(first))

    forward(0)
    notice.wait_recv()
    for q in range(5):
        band_out[1, q] = chosen(roles(1)[0], q)
    shares[1].start()
    forward(1)
    pl.when(my_half == 0)(lambda: meet(True))
    pl.when(my_half == 1)(lambda: meet(False))
    def finish(first):
        backward(first)
        backward(1 - first)

    pl.when(later)(lambda: finish(1))
    pl.when(jnp.logical_not(later))(lambda: finish(0))

    moved, stayed = zip(*[roles(p) for p in range(2)])
    for q in range(5):
        for p in range(2):
            giving(p, q).wait_recv()
        for k in range(4):
            total = jnp.zeros((100, 128), jnp.float32)
            for p in range(2):
                total = total - jnp.where(stayed[p] == float(k), kept[p, q, pl.ds(0, 100), :], 0.0)
                total = total - jnp.where(moved[p] == float(k), taken[p, q], 0.0)
            for a in range(10):
                first = (a * 5 + q) * 40 + k
                staged[pl.ds(first, 8, stride=4), :] = total[8 * a : 8 * a + 8]
                staged[pl.ds(first + 32, 2, stride=4), :] = total[80 + 2 * a : 82 + 2 * a]
        for a in range(10):
            t = a * 5 + q
            for x in range(10):
                out_ref[x, :, pl.ds(t * 128, 128)] = staged[pl.ds(t * 40 + 4 * x, 4), :]

    notice.wait_send()
    for p in range(2):
        shares[p].wait_send()
        for x, big, half in targets(p):
            going(p, x, big, half).wait_send()
        for q in range(5):
            giving(p, q).wait_send()
    for g in range(8):
        returning(g, True).wait_send()
        returning(g, False).wait_send()


def body(bands, pair_list):
    constants = [jnp.asarray(table) for table in tables()]
    f32 = jnp.float32
    dma = pltpu.SemaphoreType.DMA
    scratch = [pltpu.VMEM((10, 4, 6400), f32), pltpu.VMEM((2000, 128), f32), pltpu.VMEM((4, 5, ROWS, 128), f32)]
    scratch += [pltpu.VMEM(table.shape, table.dtype) for table in constants]
    scratch += [pltpu.VMEM((2, 5, ROWS, 128), f32)] * 2
    scratch += [pltpu.VMEM((8, 128), f32)] * 2
    scratch += [pltpu.VMEM((2, 5, ROWS, 128), f32)] * 2
    scratch += [pltpu.VMEM((2, 5, 100, 128), f32)] * 2
    big, small = 10 * BIG, 10 * SMALL
    scratch += [pltpu.VMEM((2, 4, big, 128), f32), pltpu.VMEM((2, 4, small, 128), f32)]
    scratch += [pltpu.VMEM((8, big, 128), f32), pltpu.VMEM((8, small, 128), f32)] * 2
    scratch += [pltpu.VMEM((2, 4, big, 128), f32), pltpu.VMEM((2, 4, small, 128), f32)]
    scratch += [pltpu.VMEM((NG, 128 * BIG), f32), pltpu.VMEM((NG, 128 * SMALL), f32), pltpu.VMEM((112, 768), f32)]
    scratch += [dma((10,)), dma((2, 2)), dma((2,)), dma((2, 2, 5))]
    scratch += [dma((2, 4))] * 2 + [dma((8,))] * 4 + [dma((2, 4))] * 2
    lines = bands.transpose(1, 0, 2)
    action = pl.pallas_call(
        kernel,
        out_shape=jax.ShapeDtypeStruct(lines.shape, f32),
        in_specs=[pl.BlockSpec(memory_space=pltpu.SMEM)] + [pl.BlockSpec(memory_space=pl.ANY)] * 10,
        out_specs=pl.BlockSpec(memory_space=pltpu.VMEM),
        scratch_shapes=scratch,
        compiler_params=pltpu.CompilerParams(collective_id=0, has_side_effects=True, vmem_limit_bytes=62 * 2**20),
        name="exchange",
    )(pair_list, lines, *constants)
    return action.transpose(1, 0, 2)


def solution(mesh):
    in_specs = (P("band", "grid", None), P("band", None, None, None))
    out_specs = P("band", "grid", None)
    return jax.shard_map(body, mesh=mesh, in_specs=in_specs, out_specs=out_specs, check_vma=False)
```
